32 devices in a mesh: dp: 8 (over z, y), mp: 4 (over x, core).
Axes of the slice: x: 2, y: 2, z: 4, core: 2. Of those that a mesh axis runs over, the one named last changes fastest.
Arguments:
- inputs: bfloat16 [64, 197, 768], P('dp'), may hold values from -6 to 6
- cotangent: bfloat16 [64, 197, 768], P('dp'), may hold values from -6 to 6
- counts: int32 [8], P('dp'), may hold values from 1 to 8, 36 in all
- qkv_weight: float32 [2, 768, 3, 768], P(None, 'dp', None, 'mp'), may hold values from -0.21875 to 0.21875
- out_weight: float32 [2, 768, 768], P(None, 'mp', 'dp'), may hold values from -0.875 to 0.875
- up_weight: float32 [2, 768, 3072], P(None, 'dp', 'mp'), may hold values from -0.21875 to 0.21875
- down_weight: float32 [2, 3072, 768], P(None, 'mp', 'dp'), may hold values from -0.109375 to 0.109375
- vectors: float32 [2, 4, 8, 288], P(None, 'mp', 'dp'), may hold values from 0.5 to 1.5
- qkv_first: float32 [2, 768, 3, 768], P(None, 'dp', None, 'mp'), may hold values from -48 to 48
- qkv_second: float32 [2, 768, 3, 768], P(None, 'dp', None, 'mp'), may hold values from 425.52 to 1418.4
- out_first: float32 [2, 768, 768], P(None, 'mp', 'dp'), may hold values from -48 to 48
- out_second: float32 [2, 768, 768], P(None, 'mp', 'dp'), may hold values from 425.52 to 1418.4
- up_first: float32 [2, 768, 3072], P(None, 'dp', 'mp'), may hold values from -48 to 48
- up_second: float32 [2, 768, 3072], P(None, 'dp', 'mp'), may hold values from 425.52 to 1418.4
- down_first: float32 [2, 3072, 768], P(None, 'mp', 'dp'), may hold values from -48 to 48
- down_second: float32 [2, 3072, 768], P(None, 'mp', 'dp'), may hold values from 425.52 to 1418.4
- vector_first: float32 [2, 4, 8, 288], P(None, 'mp', 'dp'), may hold values from -48 to 48
- vector_second: float32 [2, 4, 8, 288], P(None, 'mp', 'dp'), may hold values from 425.52 to 1418.4
Outputs:
- output_tokens: bfloat16 [64, 197, 768], P('dp')
- input_grad: float32 [64, 197, 768], P('dp')
- qkv_first_new: float32 [2, 768, 3, 768], P(None, 'dp', None, 'mp')
- qkv_second_new: float32 [2, 768, 3, 768], P(None, 'dp', None, 'mp')
- qkv_weight_new: float32 [2, 768, 3, 768], P(None, 'dp', None, 'mp')
- out_first_new: float32 [2, 768, 768], P(None, 'mp', 'dp')
- out_second_new: float32 [2, 768, 768], P(None, 'mp', 'dp')
- out_weight_new: float32 [2, 768, 768], P(None, 'mp', 'dp')
- up_first_new: float32 [2, 768, 3072], P(None, 'dp', 'mp')
- up_second_new: float32 [2, 768, 3072], P(None, 'dp', 'mp')
- up_weight_new: float32 [2, 768, 3072], P(None, 'dp', 'mp')
- down_first_new: float32 [2, 3072, 768], P(None, 'mp', 'dp')
- down_second_new: float32 [2, 3072, 768], P(None, 'mp', 'dp')
- down_weight_new: float32 [2, 3072, 768], P(None, 'mp', 'dp')
- vector_first_new: float32 [2, 4, 8, 288], P(None, 'mp', 'dp')
- vector_second_new: float32 [2, 4, 8, 288], P(None, 'mp', 'dp')
- vector_new: float32 [2, 4, 8, 288], P(None, 'mp', 'dp')
The draws below stay inside these ranges and needn't reach their ends.
Inputs may be any that keep to these rules, and one draw needn't show every extreme that they name: counts sums to 36, and some index of dp holds exactly 8 images.
All inputs are finite; a program needn't handle non-finite values. No bound on the sum of `counts` on one device may be relied on, other than what follows from the above.
Results may differ from the reference program's by a relative error of at most 0.017.
Values may be sent and summed in bfloat16 or wider, within the bound.
A program may use at most 192 MiB of HBM per device.

```python
import math
from functools import partial
import jax
import jax.numpy as jnp
import numpy as np
from jax import lax

D = 768
HEADS = 12
HEAD_DIM = 64
FF = 3072
LAYERS = 2
SEQ = 197
CAP = 8
STEP = 10
IMAGES = 36
SLOTS = 64
VB = 288
N_DP = 8
N_MP = 4


def block_levels(key, extent, split, smallest, high):
    def one(axis_at, blocks):
        draws = jax.random.uniform(jax.random.fold_in(jax.random.fold_in(key, 6), axis_at), (blocks,), jnp.float32, smallest / len(split), high / len(split))
        return jnp.repeat(jnp.exp(draws), extent[axis_at] // blocks).reshape((-1,) + (1,) * (len(extent) - axis_at - 1))

    loudness = one(*split[0])
    for cut in split[1:]:
        loudness = loudness * one(*cut)
    return loudness


def profile(count, total, reach, slope):
    portions = [(1 << 20) // math.isqrt(rank ** slope) + 1 for rank in range(2, count + 1)]
    spare, holding = total - reach - (count - 1), [1] * (count - 1)
    while spare > 0:
        candidates = [i for i in range(count - 1) if holding[i] < reach]
        pool, remaining = sum([portions[i] for i in candidates]), spare
        for i in candidates:
            more = min(reach - holding[i], max(1, remaining * portions[i] // pool), spare)
            holding[i] = holding[i] + more
            spare = spare - more
    return np.array([reach] + holding)


def uneven_parts(rng, amount, total, reach, skew):
    if amount == 2:
        one = jax.random.randint(rng, (), max(1, total - reach), min(reach, total - 1) + 1)
        return jnp.stack([one, total - one])
    lengths = jnp.asarray(profile(amount, total, reach, skew), jnp.int32)
    twos = (amount - 1) // 2
    source_of, receiver = lengths[1:1 + 2 * twos:2], lengths[2:2 + 2 * twos:2]
    slack = jnp.minimum(source_of - 1, reach - receiver)
    passed = jax.random.randint(jax.random.fold_in(rng, 1), (twos,), 0, 1 << 20) % (slack + 1)
    lengths = lengths.at[1:1 + 2 * twos:2].set(source_of - passed).at[2:2 + 2 * twos:2].set(receiver + passed)
    return lengths[jax.random.permutation(jax.random.fold_in(rng, 2), amount)]


def bell_draw(stream_key, dims, deviation, most, pieces=(), held_as=jnp.bfloat16):
    result = deviation * jax.random.normal(stream_key, dims, jnp.float32)
    if pieces:
        result = result * block_levels(stream_key, dims, pieces, -0.22, 0.18)
    return jnp.clip(result, -most, most).astype(held_as)


def setup_inputs(seed: int = 0) -> dict:
    splits = jax.random.split(jax.random.key(seed), 19)
    inputs = bell_draw(splits[0], (SLOTS, SEQ, D), 1.0, 6.0, ((0, 8),))
    cotangent = bell_draw(splits[1], (SLOTS, SEQ, D), 1.0, 6.0, ((0, 8),))
    counts = uneven_parts(splits[2], N_DP, IMAGES, CAP, 1).astype(jnp.int32)
    qkv_weight = bell_draw(splits[3], (LAYERS, D, 3, D), D ** -0.5, 0.21875, ((1, 8), (3, 4)), jnp.float32)
    out_weight = bell_draw(splits[4], (LAYERS, D, D), (D // 16) ** -0.5, 0.875, ((1, 4), (2, 8)), jnp.float32)
    up_weight = bell_draw(splits[5], (LAYERS, D, FF), D ** -0.5, 0.21875, ((1, 8), (2, 4)), jnp.float32)
    down_weight = bell_draw(splits[6], (LAYERS, FF, D), FF ** -0.5, 0.109375, ((1, 4), (2, 8)), jnp.float32)
    vectors = jnp.clip(0.5 + 1.0 * jax.random.uniform(splits[7], (LAYERS, N_MP, N_DP, VB), jnp.float32) ** block_levels(splits[7], (LAYERS, N_MP, N_DP, VB), ((1, 4), (2, 8)), -0.2, 0.2), 0.5, 1.5)
    qkv_first = bell_draw(splits[8], (LAYERS, D, 3, D), (0.1 * (IMAGES * SEQ) ** 0.5), 48.0, ((1, 8), (3, 4)), jnp.float32)
    qkv_second = jnp.clip(jnp.exp(math.log(1418.4) - 1.2039728 * jax.random.uniform(splits[9], (LAYERS, D, 3, D), jnp.float32) ** block_levels(splits[9], (LAYERS, D, 3, D), ((1, 8), (3, 4)), -0.2, 0.2)), 425.52, 1418.4)
    out_first = bell_draw(splits[10], (LAYERS, D, D), (0.1 * (IMAGES * SEQ) ** 0.5), 48.0, ((1, 4), (2, 8)), jnp.float32)
    out_second = jnp.clip(jnp.exp(math.log(1418.4) - 1.2039728 * jax.random.uniform(splits[11], (LAYERS, D, D), jnp.float32) ** block_levels(splits[11], (LAYERS, D, D), ((1, 4), (2, 8)), -0.2, 0.2)), 425.52, 1418.4)
    up_first = bell_draw(splits[12], (LAYERS, D, FF), (0.1 * (IMAGES * SEQ) ** 0.5), 48.0, ((1, 8), (2, 4)), jnp.float32)
    up_second = jnp.clip(jnp.exp(math.log(1418.4) - 1.2039728 * jax.random.uniform(splits[13], (LAYERS, D, FF), jnp.float32) ** block_levels(splits[13], (LAYERS, D, FF), ((1, 8), (2, 4)), -0.2, 0.2)), 425.52, 1418.4)
    down_first = bell_draw(splits[14], (LAYERS, FF, D), (0.1 * (IMAGES * SEQ) ** 0.5), 48.0, ((1, 4), (2, 8)), jnp.float32)
    down_second = jnp.clip(jnp.exp(math.log(1418.4) - 1.2039728 * jax.random.uniform(splits[15], (LAYERS, FF, D), jnp.float32) ** block_levels(splits[15], (LAYERS, FF, D), ((1, 4), (2, 8)), -0.2, 0.2)), 425.52, 1418.4)
    vector_first = bell_draw(splits[16], (LAYERS, N_MP, N_DP, VB), (0.1 * (IMAGES * SEQ) ** 0.5), 48.0, ((1, 4), (2, 8)), jnp.float32)
    vector_second = jnp.clip(jnp.exp(math.log(1418.4) - 1.2039728 * jax.random.uniform(splits[17], (LAYERS, N_MP, N_DP, VB), jnp.float32) ** block_levels(splits[17], (LAYERS, N_MP, N_DP, VB), ((1, 4), (2, 8)), -0.2, 0.2)), 425.52, 1418.4)
    return {"inputs": inputs, "cotangent": cotangent, "counts": counts, "qkv_weight": qkv_weight, "out_weight": out_weight, "up_weight": up_weight, "down_weight": down_weight, "vectors": vectors, "qkv_first": qkv_first, "qkv_second": qkv_second, "out_first": out_first, "out_second": out_second, "up_first": up_first, "up_second": up_second, "down_first": down_first, "down_second": down_second, "vector_first": vector_first, "vector_second": vector_second}


@jax.custom_vjp
def low(v):
    return lax.optimization_barrier(v.astype(jnp.bfloat16)).astype(jnp.float32)

@jax.custom_vjp
def low_back(v):
    return v

def low_keep(v):
    return (low(v), None)

def low_pass(kept, grad):
    return (grad,)

def back_keep(v):
    return (v, None)

def back_low(kept, grad):
    return (low(grad),)
low.defvjp(low_keep, low_pass)
low_back.defvjp(back_keep, back_low)

def both_round(values):
    return low(low_back(values))

def matmul_high(left, right):
    return jnp.dot(left, right, precision=lax.Precision.HIGHEST, preferred_element_type=jnp.float32)

def layer_norm(values, gain_row, shift_row):
    average = lax.optimization_barrier(jnp.mean(values, axis=-1, keepdims=True))
    centered = values - average
    variance = lax.optimization_barrier(jnp.mean(centered * centered, axis=-1, keepdims=True))
    return centered * lax.rsqrt(variance + 1e-06) * gain_row + shift_row

def attend_block(triple):
    query_rows, key_rows, value_rows = triple
    scores = jnp.einsum('bqhd,bkhd->bhqk', query_rows, key_rows, precision=lax.Precision.HIGHEST) * HEAD_DIM ** (-0.5)
    scores = low_back(scores)
    softmax_rows = low(jax.nn.softmax(scores, axis=-1))
    return jnp.einsum('bhqk,bkhd->bqhd', softmax_rows, value_rows, precision=lax.Precision.HIGHEST)

def forward_all(stream_in, qkv_weight, out_weight, up_weight, down_weight, vectors, live_slots):
    head_cols = D // N_MP
    unit_cols = FF // N_MP
    row_width = 6 * D // N_MP
    row_count = SLOTS * SEQ
    stream = stream_in.reshape(row_count, D)
    attend = jax.checkpoint(attend_block)
    for layer_index in range(LAYERS):
        blocks = vectors[layer_index].reshape(N_MP, (8 * D + FF) // N_MP)
        row_part = blocks[:, :row_width].reshape(6, D)
        normed = low(layer_norm(stream, row_part[0], row_part[1]))
        qkv_low = low(qkv_weight[layer_index])
        out_low = low(out_weight[layer_index])
        up_low = low(up_weight[layer_index])
        down_low = low(down_weight[layer_index])
        query_list, key_list, value_list = ([], [], [])
        for group_index in range(N_MP):
            columns = slice(group_index * head_cols, (group_index + 1) * head_cols)
            projected = jnp.einsum('rd,dce->rce', low_back(normed), qkv_low[:, :, columns], precision=lax.Precision.HIGHEST)
            query_list.append(both_round(projected[:, 0] + blocks[group_index, row_width:row_width + head_cols]))
            key_list.append(both_round(projected[:, 1]))
            value_list.append(both_round(projected[:, 2] + blocks[group_index, row_width + head_cols:row_width + 2 * head_cols]))
        shaped = tuple((jnp.concatenate(part_list, 1).reshape(N_DP, CAP, SEQ, HEADS, HEAD_DIM) for part_list in (query_list, key_list, value_list)))
        attended = both_round(lax.map(attend, shaped).reshape(row_count, D))
        branch = jnp.zeros((row_count, D), jnp.float32)
        for group_index in range(N_MP):
            columns = slice(group_index * head_cols, (group_index + 1) * head_cols)
            branch = branch + low(matmul_high(attended[:, columns], out_low[columns, :]))
        middle = stream + low_back(branch) + row_part[4]
        mixed = low(layer_norm(middle, row_part[2], row_part[3]))
        branch = jnp.zeros((row_count, D), jnp.float32)
        for group_index in range(N_MP):
            columns = slice(group_index * unit_cols, (group_index + 1) * unit_cols)
            hidden = low_back(matmul_high(low_back(mixed), up_low[:, columns]) + blocks[group_index, row_width + 2 * head_cols:])
            activated = low(jax.nn.gelu(hidden, approximate=False))
            branch = branch + low(matmul_high(activated, down_low[columns, :]))
        stream = middle + low_back(branch) + row_part[5]
    return stream.reshape(SLOTS, SEQ, D) * live_slots

def adam_update(weight, first_moment, second_moment, gradient, step_rate, decay_rate):
    first_new = 0.9 * first_moment + 0.1 * gradient
    second_new = 0.95 * second_moment + 0.05 * gradient * gradient
    first_hat = first_new / (1.0 - 0.9 ** STEP)
    second_hat = second_new / (1.0 - 0.95 ** STEP)
    weight_new = weight - step_rate * (first_hat / (jnp.sqrt(second_hat) + 1e-08) + decay_rate * weight)
    return (first_new, second_new, weight_new)

def reference(inputs, cotangent, counts, qkv_weight, out_weight, up_weight, down_weight, vectors, qkv_first, qkv_second, out_first, out_second, up_first, up_second, down_first, down_second, vector_first, vector_second):
    live_slots = (jnp.arange(CAP, dtype=jnp.int32)[None, :] < counts[:, None]).astype(jnp.float32).reshape(SLOTS, 1, 1)
    output, pullback = jax.vjp(partial(forward_all, live_slots=live_slots), inputs.astype(jnp.float32), qkv_weight, out_weight, up_weight, down_weight, vectors)
    input_grad, qkv_grad, out_grad, up_grad, down_grad, vector_grad = pullback(cotangent.astype(jnp.float32))
    matrix_rate = 3.0 / D ** 0.5
    qkv_new = adam_update(qkv_weight, qkv_first, qkv_second, qkv_grad, matrix_rate, 0.1)
    out_new = adam_update(out_weight, out_first, out_second, out_grad, matrix_rate, 0.1)
    up_new = adam_update(up_weight, up_first, up_second, up_grad, matrix_rate, 0.1)
    down_new = adam_update(down_weight, down_first, down_second, down_grad, matrix_rate, 0.1)
    vector_new = adam_update(vectors, vector_first, vector_second, vector_grad, 0.5, 0.0)
    return (output.astype(jnp.bfloat16), input_grad, qkv_new[0], qkv_new[1], qkv_new[2], out_new[0], out_new[1], out_new[2], up_new[0], up_new[1], up_new[2], down_new[0], down_new[1], down_new[2], vector_new[0], vector_new[1], vector_new[2])
```

```python
import functools

import jax
import jax.numpy as jnp
from jax import lax
from jax.experimental import pallas as pl
from jax.experimental.pallas import tpu as pltpu
from jax.sharding import PartitionSpec as P

D = 768
HEAD_DIM = 64
STEP = 10
ROW_TILE = 16

norm_epsilon = 1e-06
bf16 = jnp.bfloat16
f32 = jnp.float32


def norm_stats(values):
    average = jnp.mean(values, axis=-1, keepdims=True)
    centered = values - average
    variance = jnp.mean(centered * centered, axis=-1, keepdims=True)
    scale = lax.rsqrt(variance + norm_epsilon)
    return centered * scale, scale


def norm_back(values, gain_row, grad_rows):
    unit_rows, scale = norm_stats(values)
    scaled = grad_rows * gain_row
    back = scale * (
        scaled
        - jnp.mean(scaled, axis=-1, keepdims=True)
        - unit_rows * jnp.mean(scaled * unit_rows, axis=-1, keepdims=True)
    )
    return back, jnp.sum(grad_rows * unit_rows, axis=0), jnp.sum(grad_rows, axis=0)


def gelu_exact(values):
    return values * 0.5 * (1.0 + lax.erf(values * 0.5**0.5))


def gelu_slope(values):
    bell = jnp.exp(-0.5 * values * values) * (2.0 * jnp.pi) ** -0.5
    return 0.5 * (1.0 + lax.erf(values * 0.5**0.5)) + values * bell


def adam_update(weight, first_moment, second_moment, gradient, step_rate, decay_rate):
    first_new = 0.9 * first_moment + 0.1 * gradient
    second_new = 0.95 * second_moment + 0.05 * gradient * gradient
    first_hat = first_new / (1.0 - 0.9**STEP)
    second_hat = second_new / (1.0 - 0.95**STEP)
    weight_new = weight - step_rate * (
        first_hat / (jnp.sqrt(second_hat) + 1e-08) + decay_rate * weight
    )
    return (first_new, second_new, weight_new)


def dot_nn(left, right):
    return lax.dot_general(left, right, (((1,), (0,)), ((), ())), preferred_element_type=f32)


def dot_nt(left, right):
    return lax.dot_general(left, right, (((1,), (1,)), ((), ())), preferred_element_type=f32)


def dot_tn(left, right):
    return lax.dot_general(left, right, (((0,), (0,)), ((), ())), preferred_element_type=f32)


def head_probs(query, key, seq_len):
    scores = dot_nt(query, key) * HEAD_DIM ** (-0.5)
    column = lax.broadcasted_iota(jnp.int32, scores.shape, 1)
    scores = jnp.where(column < seq_len, scores, -1e30)
    raised = jnp.exp(scores - jnp.max(scores, axis=-1, keepdims=True))
    return raised * (1.0 / jnp.sum(raised, axis=-1, keepdims=True))


def attention_forward_kernel(seq_len, qkv_ref, out_ref):
    width = out_ref.shape[1]
    for at in range(0, width, HEAD_DIM):
        query = qkv_ref[:, at : at + HEAD_DIM]
        key = qkv_ref[:, width + at : width + at + HEAD_DIM]
        value = qkv_ref[:, 2 * width + at : 2 * width + at + HEAD_DIM]
        probs = head_probs(query, key, seq_len).astype(bf16)
        out_ref[:, at : at + HEAD_DIM] = dot_nn(probs, value).astype(bf16)


def attention_backward_kernel(seq_len, qkv_ref, grad_ref, out_ref):
    width = grad_ref.shape[1]
    for at in range(0, width, HEAD_DIM):
        query = qkv_ref[:, at : at + HEAD_DIM]
        key = qkv_ref[:, width + at : width + at + HEAD_DIM]
        value = qkv_ref[:, 2 * width + at : 2 * width + at + HEAD_DIM]
        grad = grad_ref[:, at : at + HEAD_DIM]
        probs = head_probs(query, key, seq_len)
        value_grad = dot_tn(probs.astype(bf16), grad)
        prob_grad = dot_nt(grad, value)
        score_grad = (
            probs * (prob_grad - jnp.sum(probs * prob_grad, axis=-1, keepdims=True))
        ).astype(bf16)
        query_grad = dot_nn(score_grad, key) * HEAD_DIM ** (-0.5)
        key_grad = dot_tn(score_grad, query) * HEAD_DIM ** (-0.5)
        out_ref[:, at : at + HEAD_DIM] = query_grad.astype(bf16)
        out_ref[:, width + at : width + at + HEAD_DIM] = key_grad.astype(bf16)
        out_ref[:, 2 * width + at : 2 * width + at + HEAD_DIM] = value_grad.astype(bf16)


def image_block(rows, columns):
    return pl.BlockSpec((rows, columns), lambda image: (image, 0))


def attention_forward(qkv_rows, images, seq_len):
    rows, width = qkv_rows.shape
    pad_len = rows // images
    return pl.pallas_call(
        functools.partial(attention_forward_kernel, seq_len),
        grid=(images,),
        in_specs=[image_block(pad_len, width)],
        out_specs=image_block(pad_len, width // 3),
        out_shape=jax.ShapeDtypeStruct((rows, width // 3), bf16),
        cost_estimate=pl.CostEstimate(
            flops=4 * rows * pad_len * (width // 3),
            bytes_accessed=rows * width * 3,
            transcendentals=rows * pad_len * (width // 3 // HEAD_DIM),
        ),
    )(qkv_rows)


def attention_backward(qkv_rows, grad_rows, images, seq_len):
    rows, width = qkv_rows.shape
    pad_len = rows // images
    return pl.pallas_call(
        functools.partial(attention_backward_kernel, seq_len),
        grid=(images,),
        in_specs=[image_block(pad_len, width), image_block(pad_len, width // 3)],
        out_specs=image_block(pad_len, width),
        out_shape=jax.ShapeDtypeStruct((rows, width), bf16),
        cost_estimate=pl.CostEstimate(
            flops=10 * rows * pad_len * (width // 3),
            bytes_accessed=rows * width * 5,
            transcendentals=rows * pad_len * (width // 3 // HEAD_DIM),
        ),
    )(qkv_rows, grad_rows)


def on_device(
    inputs,
    cotangent,
    counts,
    qkv_weight,
    out_weight,
    up_weight,
    down_weight,
    vectors,
    qkv_first,
    qkv_second,
    out_first,
    out_second,
    up_first,
    up_second,
    down_first,
    down_second,
    vector_first,
    vector_second,
):
    slot_count, seq_len, model_width = inputs.shape
    dp_count = lax.axis_size("dp")
    mp_count = lax.axis_size("mp")
    mp_index = lax.axis_index("mp")
    layers, shard_rows, _, head_cols = qkv_weight.shape
    hidden_cols = up_weight.shape[2]
    qkv_cols = 3 * head_cols
    row_width = 6 * model_width // mp_count
    half = mp_count // 2
    side = mp_index // half
    pair_swap = [(i, i ^ 1) for i in range(mp_count)]
    side_swap = [(i, (i + half) % mp_count) for i in range(mp_count)]
    own_at = mp_index
    other_at = lax.rem(mp_index + half, mp_count)
    images = slot_count // 2
    pad_len = -(-seq_len // ROW_TILE) * ROW_TILE
    rows = images * pad_len

    def to_pair(values):
        return lax.ppermute(values, "mp", pair_swap)

    def to_side(values):
        return lax.ppermute(values, "mp", side_swap)

    def pair_sum(partial_rows):
        low = partial_rows.astype(bf16)
        return low.astype(f32) + to_pair(low).astype(f32)

    vector_rows = lax.all_gather(vectors.reshape(1, -1), ("dp", "mp"), axis=0, tiled=True)
    vector_blocks = (
        vector_rows.reshape(dp_count, mp_count, layers, -1)
        .transpose(2, 1, 0, 3)
        .reshape(layers, mp_count, -1)
    )
    row_part = vector_blocks[:, :, :row_width].reshape(layers, 6, model_width)
    tails = vector_blocks[:, :, row_width:]
    tail_pair = [lax.dynamic_index_in_dim(tails, at, 1, keepdims=False) for at in (own_at, other_at)]

    def shard_pieces(layer):
        qkv_out = jnp.concatenate(
            [qkv_weight[layer].reshape(shard_rows, qkv_cols), out_weight[layer].T], axis=1
        )
        return qkv_out, up_weight[layer], down_weight[layer].T

    pieces = []
    for layer in range(layers):
        layer_pieces = []
        for piece in shard_pieces(layer):
            own = lax.all_gather(piece.astype(bf16), "dp", axis=0, tiled=True)
            layer_pieces.append((own, to_side(own)))
        pieces.append(layer_pieces)

    def own_images(values):
        mine = lax.dynamic_slice_in_dim(values, side * images, images, 0)
        mine = jnp.pad(mine, ((0, 0), (0, pad_len - seq_len), (0, 0)))
        return mine.reshape(rows, model_width).astype(f32)

    def all_images(values):
        own = values.reshape(images, pad_len, model_width)[:, :seq_len]
        other = to_side(own)
        return lax.dynamic_slice_in_dim(
            jnp.concatenate([own, other, own]), side * images, slot_count, 0
        )

    live = (
        (side * images + jnp.arange(images, dtype=jnp.int32) < counts[0])
        .astype(f32)
        .reshape(images, 1, 1)
    )

    def mask_live(values):
        return (values.reshape(images, pad_len, model_width) * live).reshape(rows, model_width)

    stream = own_images(inputs)
    kept = []
    for layer in range(layers):
        gain1, shift1, gain2, shift2, out_bias, down_bias = (row_part[layer, i] for i in range(6))
        attn_pair, up_pair, down_pair = pieces[layer]
        normed = (norm_stats(stream)[0] * gain1 + shift1).astype(bf16)
        qkv_pair, attended_pair, hidden_pair, active_pair = [], [], [], []
        branch = None
        for weight, tail in zip(attn_pair, tail_pair):
            bias = jnp.concatenate(
                [
                    tail[layer, :head_cols],
                    jnp.zeros((head_cols,), f32),
                    tail[layer, head_cols : 2 * head_cols],
                ]
            )
            qkv = (dot_nn(normed, weight[:, :qkv_cols]) + bias).astype(bf16)
            attended = attention_forward(qkv, images, seq_len)
            term = dot_nt(attended, weight[:, qkv_cols:])
            branch = term if branch is None else branch + term
            qkv_pair.append(qkv)
            attended_pair.append(attended)
        middle = stream + pair_sum(branch) + out_bias
        mixed = (norm_stats(middle)[0] * gain2 + shift2).astype(bf16)
        branch = None
        for up, down, tail in zip(up_pair, down_pair, tail_pair):
            hidden = dot_nn(mixed, up) + tail[layer, 2 * head_cols :]
            active = gelu_exact(hidden).astype(bf16)
            term = dot_nt(active, down)
            branch = term if branch is None else branch + term
            hidden_pair.append(hidden)
            active_pair.append(active)
        following = middle + pair_sum(branch) + down_bias
        kept.append((stream, normed, qkv_pair, attended_pair, middle, mixed, hidden_pair, active_pair))
        stream = following
    output_tokens = all_images(mask_live(stream).astype(bf16))

    def owner_sum(own_grad, other_grad):
        arrived = to_side(other_grad.astype(bf16))
        total = (own_grad + arrived.astype(f32)).astype(bf16)
        return lax.psum_scatter(total, "dp", scatter_dimension=0, tiled=True).astype(f32)

    upstream = mask_live(own_images(cotangent))
    grads = [None] * layers
    row_grads = [None] * layers
    column_grads = [None] * layers
    for layer in reversed(range(layers)):
        stream_in, normed, qkv_pair, attended_pair, middle, mixed, hidden_pair, active_pair = kept[
            layer
        ]
        gain1, gain2 = row_part[layer, 0], row_part[layer, 2]
        attn_pair, up_pair, down_pair = pieces[layer]
        upstream_low = upstream.astype(bf16)
        down_bias_grad = jnp.sum(upstream, axis=0)
        down_pieces, up_pieces, hidden_sums, qkv_sums = [], [], [], []
        branch = None
        for up, down, hidden, active in zip(up_pair, down_pair, hidden_pair, active_pair):
            down_pieces.append(dot_tn(upstream_low, active))
            hidden_low = (dot_nn(upstream_low, down) * gelu_slope(hidden)).astype(bf16)
            up_pieces.append(dot_tn(mixed, hidden_low))
            hidden_sums.append(jnp.sum(hidden_low.astype(f32), axis=0))
            term = dot_nt(hidden_low, up)
            branch = term if branch is None else branch + term
        mixed_grad = pair_sum(branch)
        down_grad = owner_sum(*down_pieces)
        up_grad = owner_sum(*up_pieces)
        middle_part, gain2_grad, shift2_grad = norm_back(middle, gain2, mixed_grad)
        middle_grad = upstream + middle_part
        middle_low = middle_grad.astype(bf16)
        out_bias_grad = jnp.sum(middle_grad, axis=0)
        attn_pieces = []
        branch = None
        for weight, qkv, attended in zip(attn_pair, qkv_pair, attended_pair):
            attended_grad = dot_nn(middle_low, weight[:, qkv_cols:]).astype(bf16)
            qkv_grad = attention_backward(qkv, attended_grad, images, seq_len)
            attn_pieces.append(
                jnp.concatenate([dot_tn(normed, qkv_grad), dot_tn(middle_low, attended)], axis=1)
            )
            sums = jnp.sum(qkv_grad.astype(f32), axis=0)
            qkv_sums.append(jnp.concatenate([sums[:head_cols], sums[2 * head_cols :]]))
            term = dot_nt(qkv_grad, weight[:, :qkv_cols])
            branch = term if branch is None else branch + term
        normed_grad = pair_sum(branch)
        attn_grad = owner_sum(*attn_pieces)
        stream_part, gain1_grad, shift1_grad = norm_back(stream_in, gain1, normed_grad)
        upstream = middle_grad + stream_part
        grads[layer] = (
            attn_grad[:, :qkv_cols].reshape(shard_rows, 3, head_cols),
            attn_grad[:, qkv_cols:].T,
            up_grad,
            down_grad.T,
        )
        row_grads[layer] = jnp.stack(
            [gain1_grad, shift1_grad, gain2_grad, shift2_grad, out_bias_grad, down_bias_grad]
        )
        column_grads[layer] = [
            jnp.concatenate([a, b]) for a, b in zip(qkv_sums, hidden_sums)
        ]
    input_grad = all_images(upstream.astype(bf16)).astype(f32)

    first_mask = (lax.rem(mp_index, 2) == 0).astype(f32)
    block_id = jnp.arange(mp_count, dtype=jnp.int32)
    placed = sum(
        jnp.stack([column_grads[layer][which] for layer in range(layers)])[:, None, :]
        * (block_id == at).astype(f32)[None, :, None]
        for which, at in enumerate((own_at, other_at))
    )
    row_blocks = (jnp.stack(row_grads) * first_mask).reshape(layers, mp_count, row_width)
    vector_grad = (
        jnp.concatenate([row_blocks, placed], axis=2)
        .reshape(layers, mp_count, dp_count, -1)
        .transpose(2, 1, 0, 3)
        .reshape(dp_count * mp_count, -1)
    )
    vector_grad = lax.psum_scatter(
        vector_grad, ("dp", "mp"), scatter_dimension=0, tiled=True
    ).reshape(vectors.shape)

    matrix_rate = 3.0 / D**0.5

    def update(which, weight, first, second):
        gradient = jnp.stack([grads[layer][which] for layer in range(layers)])
        return adam_update(weight, first, second, gradient, matrix_rate, 0.1)

    qkv_new = update(0, qkv_weight, qkv_first, qkv_second)
    out_new = update(1, out_weight, out_first, out_second)
    up_new = update(2, up_weight, up_first, up_second)
    down_new = update(3, down_weight, down_first, down_second)
    vector_new = adam_update(vectors, vector_first, vector_second, vector_grad, 0.5, 0.0)
    return (
        output_tokens,
        input_grad,
        qkv_new[0],
        qkv_new[1],
        qkv_new[2],
        out_new[0],
        out_new[1],
        out_new[2],
        up_new[0],
        up_new[1],
        up_new[2],
        down_new[0],
        down_new[1],
        down_new[2],
        vector_new[0],
        vector_new[1],
        vector_new[2],
    )


def solution(mesh):
    placed = (
        P("dp", None, None),
        P("dp", None, None),
        P("dp"),
        P(None, "dp", None, "mp"),
        P(None, "mp", "dp"),
        P(None, "dp", "mp"),
        P(None, "mp", "dp"),
        P(None, "mp", "dp", None),
        P(None, "dp", None, "mp"),
        P(None, "dp", None, "mp"),
        P(None, "mp", "dp"),
        P(None, "mp", "dp"),
        P(None, "dp", "mp"),
        P(None, "dp", "mp"),
        P(None, "mp", "dp"),
        P(None, "mp", "dp"),
        P(None, "mp", "dp", None),
        P(None, "mp", "dp", None),
    )
    return jax.shard_map(
        on_device,
        mesh=mesh,
        in_specs=placed,
        out_specs=(
            P("dp", None, None),
            P("dp", None, None),
            P(None, "dp", None, "mp"),
            P(None, "dp", None, "mp"),
            P(None, "dp", None, "mp"),
            P(None, "mp", "dp"),
            P(None, "mp", "dp"),
            P(None, "mp", "dp"),
            P(None, "dp", "mp"),
            P(None, "dp", "mp"),
            P(None, "dp", "mp"),
            P(None, "mp", "dp"),
            P(None, "mp", "dp"),
            P(None, "mp", "dp"),
            P(None, "mp", "dp", None),
            P(None, "mp", "dp", None),
            P(None, "mp", "dp", None),
        ),
        check_vma=False,
    )
```

```python
import functools

import jax
import jax.numpy as jnp
from jax import lax
from jax.experimental import pallas as pl
from jax.experimental.pallas import tpu as pltpu
from jax.sharding import PartitionSpec as P

D = 768
HEAD_DIM = 64
STEP = 10
ROW_TILE = 16

norm_epsilon = 1e-06
bf16 = jnp.bfloat16
f32 = jnp.float32


def norm_stats(values):
    average = jnp.mean(values, axis=-1, keepdims=True)
    centered = values - average
    variance = jnp.mean(centered * centered, axis=-1, keepdims=True)
    scale = lax.rsqrt(variance + norm_epsilon)
    return centered * scale, scale


def norm_back(values, gain_row, grad_rows):
    unit_rows, scale = norm_stats(values)
    scaled = grad_rows * gain_row
    back = scale * (
        scaled
        - jnp.mean(scaled, axis=-1, keepdims=True)
        - unit_rows * jnp.mean(scaled * unit_rows, axis=-1, keepdims=True)
    )
    return back, jnp.sum(grad_rows * unit_rows, axis=0), jnp.sum(grad_rows, axis=0)


def gelu_exact(values):
    return values * 0.5 * (1.0 + lax.erf(values * 0.5**0.5))


def gelu_slope(values):
    bell = jnp.exp(-0.5 * values * values) * (2.0 * jnp.pi) ** -0.5
    return 0.5 * (1.0 + lax.erf(values * 0.5**0.5)) + values * bell


def adam_update(weight, first_moment, second_moment, gradient, step_rate, decay_rate):
    first_new = 0.9 * first_moment + 0.1 * gradient
    second_new = 0.95 * second_moment + 0.05 * gradient * gradient
    first_hat = first_new / (1.0 - 0.9**STEP)
    second_hat = second_new / (1.0 - 0.95**STEP)
    weight_new = weight - step_rate * (
        first_hat / (jnp.sqrt(second_hat) + 1e-08) + decay_rate * weight
    )
    return (first_new, second_new, weight_new)


def dot_nn(left, right):
    return lax.dot_general(left, right, (((1,), (0,)), ((), ())), preferred_element_type=f32)


def dot_nt(left, right):
    return lax.dot_general(left, right, (((1,), (1,)), ((), ())), preferred_element_type=f32)


def dot_tn(left, right):
    return lax.dot_general(left, right, (((0,), (0,)), ((), ())), preferred_element_type=f32)


def head_probs(query, key, seq_len):
    scores = dot_nt(query, key) * HEAD_DIM ** (-0.5)
    column = lax.broadcasted_iota(jnp.int32, scores.shape, 1)
    scores = jnp.where(column < seq_len, scores, -1e30)
    raised = jnp.exp(scores - jnp.max(scores, axis=-1, keepdims=True))
    return raised * (1.0 / jnp.sum(raised, axis=-1, keepdims=True))


def attention_forward_kernel(seq_len, qkv_ref, out_ref):
    width = out_ref.shape[1]
    for at in range(0, width, HEAD_DIM):
        query = qkv_ref[:, at : at + HEAD_DIM]
        key = qkv_ref[:, width + at : width + at + HEAD_DIM]
        value = qkv_ref[:, 2 * width + at : 2 * width + at + HEAD_DIM]
        probs = head_probs(query, key, seq_len).astype(bf16)
        out_ref[:, at : at + HEAD_DIM] = dot_nn(probs, value).astype(bf16)


def attention_backward_kernel(seq_len, qkv_ref, grad_ref, out_ref):
    width = grad_ref.shape[1]
    for at in range(0, width, HEAD_DIM):
        query = qkv_ref[:, at : at + HEAD_DIM]
        key = qkv_ref[:, width + at : width + at + HEAD_DIM]
        value = qkv_ref[:, 2 * width + at : 2 * width + at + HEAD_DIM]
        grad = grad_ref[:, at : at + HEAD_DIM]
        probs = head_probs(query, key, seq_len)
        value_grad = dot_tn(probs.astype(bf16), grad)
        prob_grad = dot_nt(grad, value)
        score_grad = (
            probs * (prob_grad - jnp.sum(probs * prob_grad, axis=-1, keepdims=True))
        ).astype(bf16)
        query_grad = dot_nn(score_grad, key) * HEAD_DIM ** (-0.5)
        key_grad = dot_tn(score_grad, query) * HEAD_DIM ** (-0.5)
        out_ref[:, at : at + HEAD_DIM] = query_grad.astype(bf16)
        out_ref[:, width + at : width + at + HEAD_DIM] = key_grad.astype(bf16)
        out_ref[:, 2 * width + at : 2 * width + at + HEAD_DIM] = value_grad.astype(bf16)


def image_block(rows, columns):
    return pl.BlockSpec((rows, columns), lambda image: (image, 0))


def attention_forward(qkv_rows, images, seq_len):
    rows, width = qkv_rows.shape
    pad_len = rows // images
    return pl.pallas_call(
        functools.partial(attention_forward_kernel, seq_len),
        grid=(images,),
        in_specs=[image_block(pad_len, width)],
        out_specs=image_block(pad_len, width // 3),
        out_shape=jax.ShapeDtypeStruct((rows, width // 3), bf16),
        cost_estimate=pl.CostEstimate(
            flops=4 * rows * pad_len * (width // 3),
            bytes_accessed=rows * width * 3,
            transcendentals=rows * pad_len * (width // 3 // HEAD_DIM),
        ),
    )(qkv_rows)


def attention_backward(qkv_rows, grad_rows, images, seq_len):
    rows, width = qkv_rows.shape
    pad_len = rows // images
    return pl.pallas_call(
        functools.partial(attention_backward_kernel, seq_len),
        grid=(images,),
        in_specs=[image_block(pad_len, width), image_block(pad_len, width // 3)],
        out_specs=image_block(pad_len, width),
        out_shape=jax.ShapeDtypeStruct((rows, width), bf16),
        cost_estimate=pl.CostEstimate(
            flops=10 * rows * pad_len * (width // 3),
            bytes_accessed=rows * width * 5,
            transcendentals=rows * pad_len * (width // 3 // HEAD_DIM),
        ),
    )(qkv_rows, grad_rows)


def bit_swap(axis, bit, size):
    return [(i, i ^ (1 << bit)) for i in range(size)]


def swap_bit(values, axis, bit):
    return lax.ppermute(values, axis, bit_swap(axis, bit, lax.axis_size(axis)))


def own_bit(axis, bit):
    return lax.rem(lax.axis_index(axis) // (1 << bit), 2)


def double_bit(values, dim, axis, bit):
    other = swap_bit(values, axis, bit)
    return jnp.where(
        own_bit(axis, bit) == 0,
        jnp.concatenate([values, other], dim),
        jnp.concatenate([other, values], dim),
    )


def halve_bit(values, dim, axis, bit):
    mine = own_bit(axis, bit)
    theirs = lax.dynamic_index_in_dim(values, 1 - mine, dim, keepdims=True)
    kept = lax.dynamic_index_in_dim(values, mine, dim, keepdims=True)
    arrived = swap_bit(theirs, axis, bit)
    return (kept.astype(f32) + arrived.astype(f32)).astype(values.dtype)


def on_device(
    inputs,
    cotangent,
    counts,
    qkv_weight,
    out_weight,
    up_weight,
    down_weight,
    vectors,
    qkv_first,
    qkv_second,
    out_first,
    out_second,
    up_first,
    up_second,
    down_first,
    down_second,
    vector_first,
    vector_second,
):
    slot_count, seq_len, model_width = inputs.shape
    dp_count = lax.axis_size("dp")
    mp_count = lax.axis_size("mp")
    mp_index = lax.axis_index("mp")
    layers, shard_rows, _, head_cols = qkv_weight.shape
    hidden_cols = up_weight.shape[2]
    qkv_cols = 3 * head_cols
    row_width = 6 * model_width // mp_count
    half = mp_count // 2
    side = mp_index // half
    pair_swap = [(i, i ^ 1) for i in range(mp_count)]
    side_swap = [(i, (i + half) % mp_count) for i in range(mp_count)]
    own_at = mp_index
    other_at = lax.rem(mp_index + half, mp_count)
    images = slot_count // 2
    pad_len = -(-seq_len // ROW_TILE) * ROW_TILE
    rows = images * pad_len

    def to_pair(values):
        return lax.ppermute(values, "mp", pair_swap)

    def to_side(values):
        return lax.ppermute(values, "mp", side_swap)

    def pair_sum(partial_rows):
        low = partial_rows.astype(bf16)
        return low.astype(f32) + to_pair(low).astype(f32)

    dp_bits = dp_count.bit_length() - 1
    mp_bits = mp_count.bit_length() - 1
    dp_dims = {bit: dp_bits - 1 - bit for bit in range(dp_bits)}
    high_bits = [bit for bit in range(1, dp_bits)]

    spread = vectors.reshape((1,) * (dp_bits + mp_bits) + (layers, -1))
    for bit in range(mp_bits):
        spread = double_bit(spread, dp_bits + mp_bits - 1 - bit, "mp", bit)
    for bit in range(dp_bits):
        spread = double_bit(spread, dp_dims[bit], "dp", bit)
    vector_blocks = (
        spread.reshape(dp_count, mp_count, layers, -1)
        .transpose(2, 1, 0, 3)
        .reshape(layers, mp_count, -1)
    )
    row_part = vector_blocks[:, :, :row_width].reshape(layers, 6, model_width)
    tails = vector_blocks[:, :, row_width:]
    tail_pair = [lax.dynamic_index_in_dim(tails, at, 1, keepdims=False) for at in (own_at, other_at)]

    def gather_side_last(shard):
        held = shard.reshape((1,) * dp_bits + shard.shape)
        for bit in high_bits + [0]:
            held = double_bit(held, dp_dims[bit], "dp", bit)
        own = held.reshape(-1, shard.shape[1])
        return own, to_side(own)

    def gather_low_last(shard):
        held = shard.reshape((1,) * dp_bits + shard.shape)
        for bit in high_bits:
            held = double_bit(held, dp_dims[bit], "dp", bit)
        both = jnp.stack([held, to_side(held)])
        both = double_bit(both, 1 + dp_dims[0], "dp", 0).reshape(2, -1, shard.shape[1])
        return both[0], both[1]

    pieces = []
    for layer in range(layers):
        attn_shard = jnp.concatenate(
            [qkv_weight[layer].reshape(shard_rows, qkv_cols), out_weight[layer].T], axis=1
        ).astype(bf16)
        mlp_shard = jnp.concatenate([up_weight[layer], down_weight[layer].T], axis=1).astype(bf16)
        attn_pair = gather_side_last(attn_shard)
        mlp_pair = gather_low_last(mlp_shard)
        pieces.append(
            (
                attn_pair,
                [both[:, :hidden_cols] for both in mlp_pair],
                [both[:, hidden_cols:] for both in mlp_pair],
            )
        )

    def own_images(values):
        mine = lax.dynamic_slice_in_dim(values, side * images, images, 0)
        mine = jnp.pad(mine, ((0, 0), (0, pad_len - seq_len), (0, 0)))
        return mine.reshape(rows, model_width).astype(f32)

    def all_images(values):
        own = values.reshape(images, pad_len, model_width)[:, :seq_len]
        other = to_side(own)
        return lax.dynamic_slice_in_dim(
            jnp.concatenate([own, other, own]), side * images, slot_count, 0
        )

    live = (
        (side * images + jnp.arange(images, dtype=jnp.int32) < counts[0])
        .astype(f32)
        .reshape(images, 1, 1)
    )

    def mask_live(values):
        return (values.reshape(images, pad_len, model_width) * live).reshape(rows, model_width)

    stream = own_images(inputs)
    kept = []
    for layer in range(layers):
        gain1, shift1, gain2, shift2, out_bias, down_bias = (row_part[layer, i] for i in range(6))
        attn_pair, up_pair, down_pair = pieces[layer]
        normed = (norm_stats(stream)[0] * gain1 + shift1).astype(bf16)
        qkv_pair, attended_pair, hidden_pair, active_pair = [], [], [], []
        branch = None
        for weight, tail in zip(attn_pair, tail_pair):
            bias = jnp.concatenate(
                [
                    tail[layer, :head_cols],
                    jnp.zeros((head_cols,), f32),
                    tail[layer, head_cols : 2 * head_cols],
                ]
            )
            qkv = (dot_nn(normed, weight[:, :qkv_cols]) + bias).astype(bf16)
            attended = attention_forward(qkv, images, seq_len)
            term = dot_nt(attended, weight[:, qkv_cols:])
            branch = term if branch is None else branch + term
            qkv_pair.append(qkv)
            attended_pair.append(attended)
        middle = stream + pair_sum(branch) + out_bias
        mixed = (norm_stats(middle)[0] * gain2 + shift2).astype(bf16)
        branch = None
        for up, down, tail in zip(up_pair, down_pair, tail_pair):
            hidden = dot_nn(mixed, up) + tail[layer, 2 * head_cols :]
            active = gelu_exact(hidden).astype(bf16)
            term = dot_nt(active, down)
            branch = term if branch is None else branch + term
            hidden_pair.append(hidden)
            active_pair.append(active)
        following = middle + pair_sum(branch) + down_bias
        kept.append((stream, normed, qkv_pair, attended_pair, middle, mixed, hidden_pair, active_pair))
        stream = following
    output_tokens = all_images(mask_live(stream).astype(bf16))

    def block_dims(values):
        return values.reshape((2,) * dp_bits + (shard_rows, values.shape[-1]))

    flying = []

    def halving(bits, skip):
        return [
            functools.partial(
                lambda bit, values: halve_bit(values, skip + dp_dims[bit], "dp", bit), bit
            )
            for bit in bits
        ]

    def sum_side_first(own_grad, other_grad):
        arrived = to_side(other_grad)
        total = block_dims((own_grad.astype(f32) + arrived.astype(f32)).astype(bf16))
        flying.append([total, halving([0] + high_bits[::-1], 0)])
        return flying[-1]

    def sum_low_first(own_grad, other_grad):
        def side_step(both):
            arrived = to_side(both[1])
            return (both[0].astype(f32) + arrived.astype(f32)).astype(bf16)

        both = jnp.stack([block_dims(own_grad), block_dims(other_grad)])
        both = halve_bit(both, 1 + dp_dims[0], "dp", 0)
        flying.append([both, [side_step] + halving(high_bits[::-1], 0)])
        return flying[-1]

    def tick(values):
        active = [entry for entry in flying if entry[1]]
        values, arrived = lax.optimization_barrier((values, [entry[0] for entry in active]))
        for entry, value in zip(active, arrived):
            entry[0] = entry[1].pop(0)(value)
        return values

    def settle(entry):
        while entry[1]:
            entry[0] = entry[1].pop(0)(entry[0])
        return entry[0].reshape(shard_rows, -1).astype(f32)

    upstream = mask_live(own_images(cotangent))
    grads = [None] * layers
    row_grads = [None] * layers
    column_grads = [None] * layers
    for layer in reversed(range(layers)):
        stream_in, normed, qkv_pair, attended_pair, middle, mixed, hidden_pair, active_pair = kept[
            layer
        ]
        gain1, gain2 = row_part[layer, 0], row_part[layer, 2]
        attn_pair, up_pair, down_pair = pieces[layer]
        upstream_low = upstream.astype(bf16)
        down_bias_grad = jnp.sum(upstream, axis=0)
        down_pieces, up_pieces, hidden_sums, qkv_sums = [], [], [], []
        branch = None
        for up, down, hidden, active in zip(up_pair, down_pair, hidden_pair, active_pair):
            down_pieces.append(dot_tn(upstream_low, active).astype(bf16))
            hidden_low = (dot_nn(upstream_low, down) * gelu_slope(hidden)).astype(bf16)
            up_pieces.append(dot_tn(mixed, hidden_low).astype(bf16))
            hidden_sums.append(jnp.sum(hidden_low.astype(f32), axis=0))
            term = dot_nt(hidden_low, up)
            branch = term if branch is None else branch + term
        mixed_grad = pair_sum(tick(branch))
        mixed_grad, down_pieces, up_pieces = lax.optimization_barrier(
            (mixed_grad, down_pieces, up_pieces)
        )
        mixed_grad = tick(mixed_grad)
        down_grad = sum_side_first(*down_pieces)
        up_grad = sum_low_first(*up_pieces)
        middle_part, gain2_grad, shift2_grad = norm_back(middle, gain2, mixed_grad)
        middle_grad = upstream + middle_part
        middle_low = middle_grad.astype(bf16)
        out_bias_grad = jnp.sum(middle_grad, axis=0)
        attn_pieces = []
        branch = None
        for weight, qkv, attended in zip(attn_pair, qkv_pair, attended_pair):
            attended_grad = dot_nn(middle_low, weight[:, qkv_cols:]).astype(bf16)
            qkv_grad = attention_backward(qkv, attended_grad, images, seq_len)
            qkv_grad, middle_low = tick((qkv_grad, middle_low))
            attn_pieces.append(
                jnp.concatenate(
                    [
                        dot_tn(normed, qkv_grad).astype(bf16),
                        dot_tn(middle_low, attended).astype(bf16),
                    ],
                    axis=1,
                )
            )
            sums = jnp.sum(qkv_grad.astype(f32), axis=0)
            qkv_sums.append(jnp.concatenate([sums[:head_cols], sums[2 * head_cols :]]))
            term = dot_nt(qkv_grad, weight[:, :qkv_cols])
            branch = term if branch is None else branch + term
        normed_grad = pair_sum(branch)
        normed_grad, attn_pieces = tick((normed_grad, attn_pieces))
        cut = attn_pieces[0].shape[1] // 2
        attn_grad = [
            sum_side_first(*[piece[:, :cut] for piece in attn_pieces]),
            sum_low_first(*[piece[:, cut:] for piece in attn_pieces]),
        ]
        stream_part, gain1_grad, shift1_grad = norm_back(stream_in, gain1, normed_grad)
        upstream = middle_grad + stream_part
        grads[layer] = (attn_grad, up_grad, down_grad)
        row_grads[layer] = jnp.stack(
            [gain1_grad, shift1_grad, gain2_grad, shift2_grad, out_bias_grad, down_bias_grad]
        )
        column_grads[layer] = [
            jnp.concatenate([a, b]) for a, b in zip(qkv_sums, hidden_sums)
        ]
    input_grad = all_images(upstream.astype(bf16)).astype(f32)

    first_mask = (lax.rem(mp_index, 2) == 0).astype(f32)
    block_id = jnp.arange(mp_count, dtype=jnp.int32)
    placed = sum(
        jnp.stack([column_grads[layer][which] for layer in range(layers)])[:, None, :]
        * (block_id == at).astype(f32)[None, :, None]
        for which, at in enumerate((own_at, other_at))
    )
    row_blocks = (jnp.stack(row_grads) * first_mask).reshape(layers, mp_count, row_width)
    vector_grad = (
        jnp.concatenate([row_blocks, placed], axis=2)
        .reshape(layers, mp_count, dp_count, -1)
        .transpose(2, 1, 0, 3)
        .reshape((2,) * (dp_bits + mp_bits) + (layers, -1))
    )
    vector_grad = tick(vector_grad)
    for bit in reversed(range(dp_bits)):
        vector_grad = halve_bit(vector_grad, dp_dims[bit], "dp", bit)
    for bit in reversed(range(mp_bits)):
        vector_grad = halve_bit(vector_grad, dp_bits + mp_bits - 1 - bit, "mp", bit)
    vector_grad = vector_grad.reshape(vectors.shape)

    matrix_rate = 3.0 / D**0.5

    settled = []
    for attn_grad, up_grad, down_grad in grads:
        attn_grad = jnp.concatenate([settle(entry) for entry in attn_grad], axis=1)
        settled.append(
            (
                attn_grad[:, :qkv_cols].reshape(shard_rows, 3, head_cols),
                attn_grad[:, qkv_cols:].T,
                settle(up_grad),
                settle(down_grad).T,
            )
        )

    def update(which, weight, first, second):
        gradient = jnp.stack([settled[layer][which] for layer in range(layers)])
        return adam_update(weight, first, second, gradient, matrix_rate, 0.1)

    qkv_new = update(0, qkv_weight, qkv_first, qkv_second)
    out_new = update(1, out_weight, out_first, out_second)
    up_new = update(2, up_weight, up_first, up_second)
    down_new = update(3, down_weight, down_first, down_second)
    vector_new = adam_update(vectors, vector_first, vector_second, vector_grad, 0.5, 0.0)
    return (
        output_tokens,
        input_grad,
        qkv_new[0],
        qkv_new[1],
        qkv_new[2],
        out_new[0],
        out_new[1],
        out_new[2],
        up_new[0],
        up_new[1],
        up_new[2],
        down_new[0],
        down_new[1],
        down_new[2],
        vector_new[0],
        vector_new[1],
        vector_new[2],
    )


def solution(mesh):
    placed = (
        P("dp", None, None),
        P("dp", None, None),
        P("dp"),
        P(None, "dp", None, "mp"),
        P(None, "mp", "dp"),
        P(None, "dp", "mp"),
        P(None, "mp", "dp"),
        P(None, "mp", "dp", None),
        P(None, "dp", None, "mp"),
        P(None, "dp", None, "mp"),
        P(None, "mp", "dp"),
        P(None, "mp", "dp"),
        P(None, "dp", "mp"),
        P(None, "dp", "mp"),
        P(None, "mp", "dp"),
        P(None, "mp", "dp"),
        P(None, "mp", "dp", None),
        P(None, "mp", "dp", None),
    )
    return jax.shard_map(
        on_device,
        mesh=mesh,
        in_specs=placed,
        out_specs=(
            P("dp", None, None),
            P("dp", None, None),
            P(None, "dp", None, "mp"),
            P(None, "dp", None, "mp"),
            P(None, "dp", None, "mp"),
            P(None, "mp", "dp"),
            P(None, "mp", "dp"),
            P(None, "mp", "dp"),
            P(None, "dp", "mp"),
            P(None, "dp", "mp"),
            P(None, "dp", "mp"),
            P(None, "mp", "dp"),
            P(None, "mp", "dp"),
            P(None, "mp", "dp"),
            P(None, "mp", "dp", None),
            P(None, "mp", "dp", None),
            P(None, "mp", "dp", None),
        ),
        check_vma=False,
    )
```

```python
import functools

import jax
import jax.numpy as jnp
from jax import lax
from jax.experimental import pallas as pl
from jax.experimental.pallas import tpu as pltpu
from jax.sharding import PartitionSpec as P

D = 768
HEAD_DIM = 64
STEP = 10
ROW_TILE = 16

norm_epsilon = 1e-06
bf16 = jnp.bfloat16
f32 = jnp.float32


def norm_stats(values):
    average = jnp.mean(values, axis=-1, keepdims=True)
    centered = values - average
    variance = jnp.mean(centered * centered, axis=-1, keepdims=True)
    scale = lax.rsqrt(variance + norm_epsilon)
    return centered * scale, scale


def norm_back(values, gain_row, grad_rows):
    unit_rows, scale = norm_stats(values)
    scaled = grad_rows * gain_row
    back = scale * (
        scaled
        - jnp.mean(scaled, axis=-1, keepdims=True)
        - unit_rows * jnp.mean(scaled * unit_rows, axis=-1, keepdims=True)
    )
    return back, jnp.sum(grad_rows * unit_rows, axis=0), jnp.sum(grad_rows, axis=0)


def gelu_exact(values):
    return values * 0.5 * (1.0 + lax.erf(values * 0.5**0.5))


def gelu_slope(values):
    bell = jnp.exp(-0.5 * values * values) * (2.0 * jnp.pi) ** -0.5
    return 0.5 * (1.0 + lax.erf(values * 0.5**0.5)) + values * bell


def adam_update(weight, first_moment, second_moment, gradient, step_rate, decay_rate):
    first_new = 0.9 * first_moment + 0.1 * gradient
    second_new = 0.95 * second_moment + 0.05 * gradient * gradient
    first_hat = first_new / (1.0 - 0.9**STEP)
    second_hat = second_new / (1.0 - 0.95**STEP)
    weight_new = weight - step_rate * (
        first_hat / (jnp.sqrt(second_hat) + 1e-08) + decay_rate * weight
    )
    return (first_new, second_new, weight_new)


def dot_nn(left, right):
    return lax.dot_general(left, right, (((1,), (0,)), ((), ())), preferred_element_type=f32)


def dot_nt(left, right):
    return lax.dot_general(left, right, (((1,), (1,)), ((), ())), preferred_element_type=f32)


def dot_tn(left, right):
    return lax.dot_general(left, right, (((0,), (0,)), ((), ())), preferred_element_type=f32)


def head_probs(query, key, seq_len):
    scores = dot_nt(query, key) * HEAD_DIM ** (-0.5)
    column = lax.broadcasted_iota(jnp.int32, scores.shape, 1)
    scores = jnp.where(column < seq_len, scores, -1e30)
    raised = jnp.exp(scores - jnp.max(scores, axis=-1, keepdims=True))
    return raised * (1.0 / jnp.sum(raised, axis=-1, keepdims=True))


def attention_forward_kernel(seq_len, qkv_ref, out_ref):
    width = out_ref.shape[1]
    for at in range(0, width, HEAD_DIM):
        query = qkv_ref[:, at : at + HEAD_DIM]
        key = qkv_ref[:, width + at : width + at + HEAD_DIM]
        value = qkv_ref[:, 2 * width + at : 2 * width + at + HEAD_DIM]
        probs = head_probs(query, key, seq_len).astype(bf16)
        out_ref[:, at : at + HEAD_DIM] = dot_nn(probs, value).astype(bf16)


def attention_backward_kernel(seq_len, qkv_ref, grad_ref, out_ref):
    width = grad_ref.shape[1]
    for at in range(0, width, HEAD_DIM):
        query = qkv_ref[:, at : at + HEAD_DIM]
        key = qkv_ref[:, width + at : width + at + HEAD_DIM]
        value = qkv_ref[:, 2 * width + at : 2 * width + at + HEAD_DIM]
        grad = grad_ref[:, at : at + HEAD_DIM]
        probs = head_probs(query, key, seq_len)
        value_grad = dot_tn(probs.astype(bf16), grad)
        prob_grad = dot_nt(grad, value)
        score_grad = (
            probs * (prob_grad - jnp.sum(probs * prob_grad, axis=-1, keepdims=True))
        ).astype(bf16)
        query_grad = dot_nn(score_grad, key) * HEAD_DIM ** (-0.5)
        key_grad = dot_tn(score_grad, query) * HEAD_DIM ** (-0.5)
        out_ref[:, at : at + HEAD_DIM] = query_grad.astype(bf16)
        out_ref[:, width + at : width + at + HEAD_DIM] = key_grad.astype(bf16)
        out_ref[:, 2 * width + at : 2 * width + at + HEAD_DIM] = value_grad.astype(bf16)


def image_block(rows, columns):
    return pl.BlockSpec((rows, columns), lambda image: (image, 0))


def attention_forward(qkv_rows, images, seq_len):
    rows, width = qkv_rows.shape
    pad_len = rows // images
    return pl.pallas_call(
        functools.partial(attention_forward_kernel, seq_len),
        grid=(images,),
        in_specs=[image_block(pad_len, width)],
        out_specs=image_block(pad_len, width // 3),
        out_shape=jax.ShapeDtypeStruct((rows, width // 3), bf16),
        cost_estimate=pl.CostEstimate(
            flops=4 * rows * pad_len * (width // 3),
            bytes_accessed=rows * width * 3,
            transcendentals=rows * pad_len * (width // 3 // HEAD_DIM),
        ),
    )(qkv_rows)


def attention_backward(qkv_rows, grad_rows, images, seq_len):
    rows, width = qkv_rows.shape
    pad_len = rows // images
    return pl.pallas_call(
        functools.partial(attention_backward_kernel, seq_len),
        grid=(images,),
        in_specs=[image_block(pad_len, width), image_block(pad_len, width // 3)],
        out_specs=image_block(pad_len, width),
        out_shape=jax.ShapeDtypeStruct((rows, width), bf16),
        cost_estimate=pl.CostEstimate(
            flops=10 * rows * pad_len * (width // 3),
            bytes_accessed=rows * width * 5,
            transcendentals=rows * pad_len * (width // 3 // HEAD_DIM),
        ),
    )(qkv_rows, grad_rows)


def bit_swap(axis, bit, size):
    return [(i, i ^ (1 << bit)) for i in range(size)]


def swap_bit(values, axis, bit):
    return lax.ppermute(values, axis, bit_swap(axis, bit, lax.axis_size(axis)))


def own_bit(axis, bit):
    return lax.rem(lax.axis_index(axis) // (1 << bit), 2)


def double_bit(values, dim, axis, bit):
    other = swap_bit(values, axis, bit)
    return jnp.where(
        own_bit(axis, bit) == 0,
        jnp.concatenate([values, other], dim),
        jnp.concatenate([other, values], dim),
    )


def halve_bit(values, dim, axis, bit):
    mine = own_bit(axis, bit)
    theirs = lax.dynamic_index_in_dim(values, 1 - mine, dim, keepdims=True)
    kept = lax.dynamic_index_in_dim(values, mine, dim, keepdims=True)
    arrived = swap_bit(theirs, axis, bit)
    return (kept.astype(f32) + arrived.astype(f32)).astype(values.dtype)


def on_device(
    inputs,
    cotangent,
    counts,
    qkv_weight,
    out_weight,
    up_weight,
    down_weight,
    vectors,
    qkv_first,
    qkv_second,
    out_first,
    out_second,
    up_first,
    up_second,
    down_first,
    down_second,
    vector_first,
    vector_second,
):
    slot_count, seq_len, model_width = inputs.shape
    dp_count = lax.axis_size("dp")
    mp_count = lax.axis_size("mp")
    mp_index = lax.axis_index("mp")
    layers, shard_rows, _, head_cols = qkv_weight.shape
    hidden_cols = up_weight.shape[2]
    qkv_cols = 3 * head_cols
    row_width = 6 * model_width // mp_count
    half = mp_count // 2
    side = mp_index // half
    pair_swap = [(i, i ^ 1) for i in range(mp_count)]
    side_swap = [(i, (i + half) % mp_count) for i in range(mp_count)]
    own_at = mp_index
    other_at = lax.rem(mp_index + half, mp_count)
    images = slot_count // 2
    pad_len = -(-seq_len // ROW_TILE) * ROW_TILE
    rows = images * pad_len

    def to_pair(values):
        return lax.ppermute(values, "mp", pair_swap)

    def to_side(values):
        return lax.ppermute(values, "mp", side_swap)

    def pair_sum(partial_rows):
        low = partial_rows.astype(bf16)
        return low.astype(f32) + to_pair(low).astype(f32)

    dp_bits = dp_count.bit_length() - 1
    mp_bits = mp_count.bit_length() - 1
    dp_dims = {bit: dp_bits - 1 - bit for bit in range(dp_bits)}
    high_bits = [bit for bit in range(1, dp_bits)]

    spread = vectors.reshape((1,) * (dp_bits + mp_bits) + (layers, -1))
    for bit in range(mp_bits):
        spread = double_bit(spread, dp_bits + mp_bits - 1 - bit, "mp", bit)
    for bit in range(dp_bits):
        spread = double_bit(spread, dp_dims[bit], "dp", bit)
    vector_blocks = (
        spread.reshape(dp_count, mp_count, layers, -1)
        .transpose(2, 1, 0, 3)
        .reshape(layers, mp_count, -1)
    )
    row_part = vector_blocks[:, :, :row_width].reshape(layers, 6, model_width)
    tails = vector_blocks[:, :, row_width:]
    tail_pair = [lax.dynamic_index_in_dim(tails, at, 1, keepdims=False) for at in (own_at, other_at)]

    def gather_side_last(shard):
        held = shard.reshape((1,) * dp_bits + shard.shape)
        for bit in high_bits + [0]:
            held = double_bit(held, dp_dims[bit], "dp", bit)
        own = held.reshape(-1, shard.shape[1])
        return own, to_side(own)

    def gather_low_last(shard):
        held = shard.reshape((1,) * dp_bits + shard.shape)
        for bit in high_bits:
            held = double_bit(held, dp_dims[bit], "dp", bit)
        both = jnp.stack([held, to_side(held)])
        both = double_bit(both, 1 + dp_dims[0], "dp", 0).reshape(2, -1, shard.shape[1])
        return both[0], both[1]

    pieces = []
    for layer in range(layers):
        attn_shard = jnp.concatenate(
            [qkv_weight[layer].reshape(shard_rows, qkv_cols), out_weight[layer].T], axis=1
        ).astype(bf16)
        mlp_shard = jnp.concatenate([up_weight[layer], down_weight[layer].T], axis=1).astype(bf16)
        if layer:
            (own, side_own), up_pair, down_pair = pieces[0]
            own, attn_shard, mlp_shard = lax.optimization_barrier((own, attn_shard, mlp_shard))
            pieces[0] = ((own, side_own), up_pair, down_pair)
        attn_pair = gather_side_last(attn_shard)
        mlp_pair = gather_low_last(mlp_shard)
        pieces.append(
            (
                attn_pair,
                [both[:, :hidden_cols] for both in mlp_pair],
                [both[:, hidden_cols:] for both in mlp_pair],
            )
        )

    def own_images(values):
        mine = lax.dynamic_slice_in_dim(values, side * images, images, 0)
        mine = jnp.pad(mine, ((0, 0), (0, pad_len - seq_len), (0, 0)))
        return mine.reshape(rows, model_width).astype(f32)

    def all_images(values):
        own = values.reshape(images, pad_len, model_width)[:, :seq_len]
        other = to_side(own)
        return lax.dynamic_slice_in_dim(
            jnp.concatenate([own, other, own]), side * images, slot_count, 0
        )

    live = (
        (side * images + jnp.arange(images, dtype=jnp.int32) < counts[0])
        .astype(f32)
        .reshape(images, 1, 1)
    )

    def mask_live(values):
        return (values.reshape(images, pad_len, model_width) * live).reshape(rows, model_width)

    stream = own_images(inputs)
    kept = []
    for layer in range(layers):
        gain1, shift1, gain2, shift2, out_bias, down_bias = (row_part[layer, i] for i in range(6))
        attn_pair, up_pair, down_pair = pieces[layer]
        normed = (norm_stats(stream)[0] * gain1 + shift1).astype(bf16)
        qkv_pair, attended_pair, hidden_pair, active_pair = [], [], [], []
        branch = None
        for weight, tail in zip(attn_pair, tail_pair):
            bias = jnp.concatenate(
                [
                    tail[layer, :head_cols],
                    jnp.zeros((head_cols,), f32),
                    tail[layer, head_cols : 2 * head_cols],
                ]
            )
            qkv = (dot_nn(normed, weight[:, :qkv_cols]) + bias).astype(bf16)
            attended = attention_forward(qkv, images, seq_len)
            term = dot_nt(attended, weight[:, qkv_cols:])
            branch = term if branch is None else branch + term
            qkv_pair.append(qkv)
            attended_pair.append(attended)
        middle = stream + pair_sum(branch) + out_bias
        mixed = (norm_stats(middle)[0] * gain2 + shift2).astype(bf16)
        branch = None
        for up, down, tail in zip(up_pair, down_pair, tail_pair):
            hidden = dot_nn(mixed, up) + tail[layer, 2 * head_cols :]
            active = gelu_exact(hidden).astype(bf16)
            term = dot_nt(active, down)
            branch = term if branch is None else branch + term
            hidden_pair.append(hidden)
            active_pair.append(active)
        following = middle + pair_sum(branch) + down_bias
        kept.append((stream, normed, qkv_pair, attended_pair, middle, mixed, hidden_pair, active_pair))
        stream = following
    output_tokens = all_images(mask_live(stream).astype(bf16))

    def block_dims(values):
        return values.reshape((2,) * dp_bits + (shard_rows, values.shape[-1]))

    flying = []

    def halving(bits, skip):
        return [
            functools.partial(
                lambda bit, values: halve_bit(values, skip + dp_dims[bit], "dp", bit), bit
            )
            for bit in bits
        ]

    def sum_side_first(own_grad, other_grad):
        arrived = to_side(other_grad)
        total = block_dims((own_grad.astype(f32) + arrived.astype(f32)).astype(bf16))
        flying.append([total, halving([0] + high_bits[::-1], 0)])
        return flying[-1]

    def sum_low_first(own_grad, other_grad):
        def side_step(both):
            arrived = to_side(both[1])
            return (both[0].astype(f32) + arrived.astype(f32)).astype(bf16)

        both = jnp.stack([block_dims(own_grad), block_dims(other_grad)])
        both = halve_bit(both, 1 + dp_dims[0], "dp", 0)
        flying.append([both, [side_step] + halving(high_bits[::-1], 0)])
        return flying[-1]

    def tick(values):
        active = [entry for entry in flying if entry[1]]
        values, arrived = lax.optimization_barrier((values, [entry[0] for entry in active]))
        for entry, value in zip(active, arrived):
            entry[0] = entry[1].pop(0)(value)
        return values

    def settle(entry):
        while entry[1]:
            entry[0] = entry[1].pop(0)(entry[0])
        return entry[0].reshape(shard_rows, -1).astype(f32)

    upstream = mask_live(own_images(cotangent))
    grads = [None] * layers
    row_grads = [None] * layers
    column_grads = [None] * layers
    for layer in reversed(range(layers)):
        stream_in, normed, qkv_pair, attended_pair, middle, mixed, hidden_pair, active_pair = kept[
            layer
        ]
        gain1, gain2 = row_part[layer, 0], row_part[layer, 2]
        attn_pair, up_pair, down_pair = pieces[layer]
        upstream_low = upstream.astype(bf16)
        down_bias_grad = jnp.sum(upstream, axis=0)
        down_pieces, up_pieces, hidden_sums, qkv_sums = [], [], [], []
        branch = None
        for up, down, hidden, active in zip(up_pair, down_pair, hidden_pair, active_pair):
            down_pieces.append(dot_tn(upstream_low, active).astype(bf16))
            hidden_low = (dot_nn(upstream_low, down) * gelu_slope(hidden)).astype(bf16)
            up_pieces.append(dot_tn(mixed, hidden_low).astype(bf16))
            hidden_sums.append(jnp.sum(hidden_low.astype(f32), axis=0))
            term = dot_nt(hidden_low, up)
            branch = term if branch is None else branch + term
        mixed_grad = pair_sum(tick(branch))
        mixed_grad, down_pieces, up_pieces = lax.optimization_barrier(
            (mixed_grad, down_pieces, up_pieces)
        )
        mixed_grad = tick(mixed_grad)
        down_grad = sum_side_first(*down_pieces)
        up_grad = sum_low_first(*up_pieces)
        middle_part, gain2_grad, shift2_grad = norm_back(middle, gain2, mixed_grad)
        middle_grad = upstream + middle_part
        middle_low = middle_grad.astype(bf16)
        out_bias_grad = jnp.sum(middle_grad, axis=0)
        attn_pieces = []
        branch = None
        for weight, qkv, attended in zip(attn_pair, qkv_pair, attended_pair):
            attended_grad = dot_nn(middle_low, weight[:, qkv_cols:]).astype(bf16)
            qkv_grad = attention_backward(qkv, attended_grad, images, seq_len)
            qkv_grad, middle_low = tick((qkv_grad, middle_low))
            attn_pieces.append(
                jnp.concatenate(
                    [
                        dot_tn(normed, qkv_grad).astype(bf16),
                        dot_tn(middle_low, attended).astype(bf16),
                    ],
                    axis=1,
                )
            )
            sums = jnp.sum(qkv_grad.astype(f32), axis=0)
            qkv_sums.append(jnp.concatenate([sums[:head_cols], sums[2 * head_cols :]]))
            term = dot_nt(qkv_grad, weight[:, :qkv_cols])
            branch = term if branch is None else branch + term
        normed_grad = pair_sum(branch)
        normed_grad, attn_pieces = tick((normed_grad, attn_pieces))
        cut = attn_pieces[0].shape[1] // 2
        attn_grad = [
            sum_side_first(*[piece[:, :cut] for piece in attn_pieces]),
            sum_low_first(*[piece[:, cut:] for piece in attn_pieces]),
        ]
        stream_part, gain1_grad, shift1_grad = norm_back(stream_in, gain1, normed_grad)
        upstream = middle_grad + stream_part
        grads[layer] = (attn_grad, up_grad, down_grad)
        row_grads[layer] = jnp.stack(
            [gain1_grad, shift1_grad, gain2_grad, shift2_grad, out_bias_grad, down_bias_grad]
        )
        column_grads[layer] = [
            jnp.concatenate([a, b]) for a, b in zip(qkv_sums, hidden_sums)
        ]
    input_grad = all_images(upstream.astype(bf16)).astype(f32)

    first_mask = (lax.rem(mp_index, 2) == 0).astype(f32)
    block_id = jnp.arange(mp_count, dtype=jnp.int32)
    placed = sum(
        jnp.stack([column_grads[layer][which] for layer in range(layers)])[:, None, :]
        * (block_id == at).astype(f32)[None, :, None]
        for which, at in enumerate((own_at, other_at))
    )
    row_blocks = (jnp.stack(row_grads) * first_mask).reshape(layers, mp_count, row_width)
    vector_grad = (
        jnp.concatenate([row_blocks, placed], axis=2)
        .reshape(layers, mp_count, dp_count, -1)
        .transpose(2, 1, 0, 3)
        .reshape((2,) * (dp_bits + mp_bits) + (layers, -1))
    )
    vector_grad = tick(vector_grad)
    for bit in reversed(range(dp_bits)):
        vector_grad = halve_bit(vector_grad, dp_dims[bit], "dp", bit)
    for bit in reversed(range(mp_bits)):
        vector_grad = halve_bit(vector_grad, dp_bits + mp_bits - 1 - bit, "mp", bit)
    vector_grad = vector_grad.reshape(vectors.shape)

    matrix_rate = 3.0 / D**0.5

    settled = []
    for attn_grad, up_grad, down_grad in grads:
        attn_grad = jnp.concatenate([settle(entry) for entry in attn_grad], axis=1)
        settled.append(
            (
                attn_grad[:, :qkv_cols].reshape(shard_rows, 3, head_cols),
                attn_grad[:, qkv_cols:].T,
                settle(up_grad),
                settle(down_grad).T,
            )
        )

    def update(which, weight, first, second):
        gradient = jnp.stack([settled[layer][which] for layer in range(layers)])
        return adam_update(weight, first, second, gradient, matrix_rate, 0.1)

    qkv_new = update(0, qkv_weight, qkv_first, qkv_second)
    out_new = update(1, out_weight, out_first, out_second)
    up_new = update(2, up_weight, up_first, up_second)
    down_new = update(3, down_weight, down_first, down_second)
    vector_new = adam_update(vectors, vector_first, vector_second, vector_grad, 0.5, 0.0)
    return (
        output_tokens,
        input_grad,
        qkv_new[0],
        qkv_new[1],
        qkv_new[2],
        out_new[0],
        out_new[1],
        out_new[2],
        up_new[0],
        up_new[1],
        up_new[2],
        down_new[0],
        down_new[1],
        down_new[2],
        vector_new[0],
        vector_new[1],
        vector_new[2],
    )


def solution(mesh):
    placed = (
        P("dp", None, None),
        P("dp", None, None),
        P("dp"),
        P(None, "dp", None, "mp"),
        P(None, "mp", "dp"),
        P(None, "dp", "mp"),
        P(None, "mp", "dp"),
        P(None, "mp", "dp", None),
        P(None, "dp", None, "mp"),
        P(None, "dp", None, "mp"),
        P(None, "mp", "dp"),
        P(None, "mp", "dp"),
        P(None, "dp", "mp"),
        P(None, "dp", "mp"),
        P(None, "mp", "dp"),
        P(None, "mp", "dp"),
        P(None, "mp", "dp", None),
        P(None, "mp", "dp", None),
    )
    return jax.shard_map(
        on_device,
        mesh=mesh,
        in_specs=placed,
        out_specs=(
            P("dp", None, None),
            P("dp", None, None),
            P(None, "dp", None, "mp"),
            P(None, "dp", None, "mp"),
            P(None, "dp", None, "mp"),
            P(None, "mp", "dp"),
            P(None, "mp", "dp"),
            P(None, "mp", "dp"),
            P(None, "dp", "mp"),
            P(None, "dp", "mp"),
            P(None, "dp", "mp"),
            P(None, "mp", "dp"),
            P(None, "mp", "dp"),
            P(None, "mp", "dp"),
            P(None, "mp", "dp", None),
            P(None, "mp", "dp", None),
            P(None, "mp", "dp", None),
        ),
        check_vma=False,
    )
```
